32 devices in a mesh: comp: 8 (over z, y), tile: 4 (over x, core).
Axes of the slice: x: 2, y: 2, z: 4, core: 2. Of those that a mesh axis runs over, the one named last changes fastest.
Arguments:
- spectrum: float32 [1152, 8192], P('comp', 'tile'), may hold values from 0.015 to 18, as said below
- depth: float32 [8192], P('tile'), may hold values from 5 to 4000
- currents: float32 [2, 8192], P(None, 'tile'), may hold values from -3 to 3
- winds: float32 [2, 8192], P(None, 'tile'), may hold values from -24 to 24
- sea_mask: int32 [8192], P('tile'), may hold values from 0 to 1
- neighbours: int32 [4, 8192], P(None, 'tile'), may hold values from 0 to 2304, as said below
- interaction: bfloat16 [1152, 1152], replicated, may hold values from -0.1875 to 0.1875
Outputs:
- spectrum_next: float32 [1152, 8192], P('comp', 'tile')
The draws below stay inside these ranges and needn't reach their ends.
Inputs may be any that keep to these rules, and one draw needn't show every extreme that they name: `spectrum`: positive everywhere. `neighbours`: for a cell at position q within its tile, entry j is either the fixed position 128 + q + 1, 128 + q - 1, 256 + q or q (for j = 0, 1, 2, 3), when that neighbour is a sea cell inside the grid, or else 2048 + 2 * 128.
All inputs are finite; a program needn't handle non-finite values.
Results may differ from the reference program's by a relative error of at most 0.00039.
The reference program's roundings to bfloat16 on the way count: a program that leaves them out, or rounds other values in their place, can miss the bound.
Values sent between devices are 32-bit elements; how exact they have to be, the bound alone decides.
A program may use at most 64 MiB of HBM per device.

```python
import math
import jax
import jax.numpy as jnp
from jax import lax

ND = 36
NF = 32
GW = 128
K = 1152
PT = 2048
NP = 8192


def grid_sea(key):
    return (jax.random.randint(key, (NP,), 0, 5) != 0).astype(jnp.int32)


def draw_sea_mask(key, part):
    return grid_sea(key)


def draw_neighbours(key, part):
    sea = grid_sea(key)
    cell = jnp.arange(NP, dtype=jnp.int32)
    local = cell % PT
    column = local % GW
    row = cell // GW
    rows = NP // GW
    sea_pad = jnp.concatenate([jnp.zeros((GW,), jnp.int32), sea, jnp.zeros((GW,), jnp.int32)])
    empty = PT + 2 * GW
    valid = [(column + 1 < GW) & (sea_pad[cell + GW + 1] == 1), (column >= 1) & (sea_pad[cell + GW - 1] == 1), (row + 1 < rows) & (sea_pad[cell + 2 * GW] == 1), (row >= 1) & (sea_pad[cell] == 1)]
    target = [GW + local + 1, GW + local - 1, 2 * GW + local, local]
    return jnp.stack([jnp.where(valid[j], target[j], empty) for j in range(4)]).astype(jnp.int32)


def draw_spectrum(key, part):
    key = jax.random.fold_in(key, 11)
    key_cell, key_comp, key_rough = jax.random.split(key, 3)
    total = NF * ND
    cell_scale = jnp.exp(jax.random.uniform(key_cell, (1, NP), jnp.float32, jnp.log(0.3), jnp.log(3.0)))
    rough = jnp.exp(jax.random.uniform(key_rough, (total, NP), jnp.float32, jnp.log(0.5), jnp.log(2.0)))
    comp_scale = jnp.exp(jax.random.uniform(key_comp, (total, 1), jnp.float32, jnp.log(0.3), jnp.log(3.0)))
    return (cell_scale * comp_scale * rough).astype(jnp.float32)


def shard_levels(stream_key, dims, shards, least, high):
    level, own = 1.0, jax.random.fold_in(stream_key, 6)
    for dim, parts in shards:
        steps = jnp.exp(jax.random.uniform(jax.random.fold_in(own, dim), (parts,), jnp.float32, least / len(shards), high / len(shards)))
        level = level * jnp.repeat(steps, dims[dim] // parts).reshape([-1 if axis == dim else 1 for axis in range(len(dims))])
    return level


def scatter_about(stream_key, extent, scale, reach, cuts=(), kind=jnp.bfloat16):
    array = scale * jax.random.normal(stream_key, extent, jnp.float32)
    if cuts:
        array = array * shard_levels(stream_key, extent, cuts, -0.22, 0.18)
    return jnp.clip(array, -reach, reach).astype(kind)


def setup_inputs(seed: int = 0) -> dict:
    seeds = jax.random.split(jax.random.key(seed), 8)
    spectrum = draw_spectrum(jax.random.fold_in(seeds[7], 71), 0)
    depth = jnp.clip(jnp.exp(math.log(4000.0) - 6.684612 * jax.random.uniform(seeds[1], (NP,), jnp.float32) ** shard_levels(seeds[1], (NP,), ((0, 4),), -0.2, 0.2)), 5.0, 4000.0)
    currents = scatter_about(seeds[2], (2, NP), 0.5, 3.0, ((1, 4),), jnp.float32)
    winds = scatter_about(seeds[3], (2, NP), 8.0, 24.0, ((1, 4),), jnp.float32)
    sea_mask = draw_sea_mask(jax.random.fold_in(seeds[7], 71), 0)
    neighbours = draw_neighbours(jax.random.fold_in(seeds[7], 71), 0)
    interaction = scatter_about(seeds[6], (K, K), K ** -0.5, 0.1875)
    return dict(spectrum=spectrum, depth=depth, currents=currents, winds=winds, sea_mask=sea_mask, neighbours=neighbours, interaction=interaction)


GRAV = 9.81
BASE_FREQ = 0.035
FREQ_RATIO = 1.1
CELL = 5000.0
STEP = 40.0
REFR_LIMIT = 0.5
WIND_RATE = 0.05
DISS_RATE = 0.3
NONLIN_RATE = 0.1

def bins(kidx):
    band = (kidx // ND).astype(jnp.float32)
    angle_id = (kidx % ND).astype(jnp.float32)
    sigma = 2.0 * math.pi * BASE_FREQ * FREQ_RATIO ** band
    theta = 2.0 * math.pi * angle_id / ND
    return (sigma, jnp.cos(theta), jnp.sin(theta))

def wave_terms(sigma, water):
    scaled = sigma * sigma / GRAV * water
    kh = scaled / jnp.tanh(scaled ** 0.75) ** (2.0 / 3.0)
    decay = jnp.exp(-2.0 * kh)
    denom = 1.0 - decay * decay
    cphase = sigma * water / kh
    cgroup = 0.5 * cphase * (1.0 + 4.0 * kh * decay / denom)
    refr = 2.0 * sigma * decay / denom
    return (cphase, cgroup, refr)

def transport(energy, vel_x, vel_y, e_nb, v_nb, live):
    u_east = 0.5 * (vel_x + v_nb[0])
    f_east = live[0] * (jnp.maximum(u_east, 0.0) * energy + jnp.minimum(u_east, 0.0) * e_nb[0])
    u_west = 0.5 * (v_nb[1] + vel_x)
    f_west = live[1] * (jnp.maximum(u_west, 0.0) * e_nb[1] + jnp.minimum(u_west, 0.0) * energy)
    u_north = 0.5 * (vel_y + v_nb[2])
    f_north = live[2] * (jnp.maximum(u_north, 0.0) * energy + jnp.minimum(u_north, 0.0) * e_nb[2])
    u_south = 0.5 * (v_nb[3] + vel_y)
    f_south = live[3] * (jnp.maximum(u_south, 0.0) * e_nb[3] + jnp.minimum(u_south, 0.0) * energy)
    return energy - STEP / CELL * (f_east - f_west + f_north - f_south)

def sources(energy, water, grad_x, grad_y, wind, mask, interaction):
    total = NF * ND
    width = energy.shape[1]
    sigma, cosine, sine = bins(jnp.arange(total, dtype=jnp.int32))
    cphase, cgroup, refr = wave_terms(sigma[:, None], water[None, :])
    ctheta = -refr * (sine[:, None] * grad_x[None, :] - cosine[:, None] * grad_y[None, :])
    rate = jnp.clip(STEP / (2.0 * math.pi / ND) * ctheta, -REFR_LIMIT, REFR_LIMIT)
    rate3 = rate.reshape(NF, ND, width)
    energy3 = energy.reshape(NF, ND, width)
    face = 0.5 * (rate3 + jnp.roll(rate3, -1, axis=1))
    flow = jnp.maximum(face, 0.0) * energy3 + jnp.minimum(face, 0.0) * jnp.roll(energy3, -1, axis=1)
    refracted = (energy3 - (flow - jnp.roll(flow, 1, axis=1))).reshape(total, width)
    squared = refracted * refracted
    rms = jnp.sqrt(lax.optimization_barrier(jnp.mean(squared, axis=0)) + 1e-06)
    fbar = lax.optimization_barrier(jnp.sum(sigma[:, None] * squared, axis=0)) / (lax.optimization_barrier(jnp.sum(squared, axis=0)) + 1e-06)
    dissipation = DISS_RATE * (sigma[:, None] / fbar[None, :]) ** 2 * (rms / (1.0 + rms))[None, :]
    drive = (wind[0][None, :] * cosine[:, None] + wind[1][None, :] * sine[:, None]) / cphase - 1.0
    gain = WIND_RATE * sigma[:, None] * jnp.maximum(drive, 0.0)
    nonlinear = jnp.dot(interaction, squared.astype(jnp.bfloat16), preferred_element_type=jnp.float32)
    updated = refracted * (1.0 + gain) + NONLIN_RATE * nonlinear / rms[None, :]
    return mask.astype(jnp.float32)[None, :] * updated / (1.0 + dissipation)

def reference(spectrum, depth, currents, winds, sea_mask, neighbours, interaction):
    total = NF * ND
    cells = spectrum.shape[1]
    empty = PT + 2 * GW
    tile_of = jnp.arange(cells, dtype=jnp.int32) // PT
    global_idx = jnp.where(neighbours == empty, cells, neighbours - GW + tile_of[None, :] * PT).astype(jnp.int32)
    live = (neighbours != empty).astype(jnp.float32)
    depth_pad = jnp.concatenate([depth, depth[:1]])
    flow_pad = jnp.concatenate([currents, currents[:, :1]], axis=1)
    near_depth = [jnp.where(live[j] > 0.0, depth_pad[global_idx[j]], depth) for j in range(4)]
    grad_x = (near_depth[0] - near_depth[1]) / (2.0 * CELL)
    grad_y = (near_depth[2] - near_depth[3]) / (2.0 * CELL)

    def advect_band(band):
        kidx = band * ND + jnp.arange(ND, dtype=jnp.int32)
        energy = lax.dynamic_slice_in_dim(spectrum, (band * ND).astype(jnp.int32), ND, 0)
        sigma, cosine, sine = bins(kidx)
        cphase, cgroup, refr = wave_terms(sigma[:, None], depth_pad[None, :])
        vel_x = cgroup * cosine[:, None] + flow_pad[0][None, :]
        vel_y = cgroup * sine[:, None] + flow_pad[1][None, :]
        e_pad = jnp.concatenate([energy, jnp.zeros((ND, 1), jnp.float32)], axis=1)
        e_nb = [e_pad[:, global_idx[j]] for j in range(4)]
        v_nb = [vel_x[:, global_idx[0]], vel_x[:, global_idx[1]], vel_y[:, global_idx[2]], vel_y[:, global_idx[3]]]
        return transport(energy, vel_x[:, :cells], vel_y[:, :cells], e_nb, v_nb, live)
    advected = lax.map(advect_band, jnp.arange(NF, dtype=jnp.int32)).reshape(total, cells)
    blocks = cells // PT
    adv_blocks = advected.reshape(total, blocks, PT).transpose(1, 0, 2)
    wind_blocks = winds.reshape(2, blocks, PT).transpose(1, 0, 2)

    def one_tile(items):
        return sources(items[0], items[1], items[2], items[3], items[4], items[5], interaction)
    result = lax.map(one_tile, (adv_blocks, depth.reshape(blocks, PT), grad_x.reshape(blocks, PT), grad_y.reshape(blocks, PT), wind_blocks, sea_mask.reshape(blocks, PT)))
    return result.transpose(1, 0, 2).reshape(total, cells)
```

```python
import functools
import math

import jax
import jax.numpy as jnp
import numpy as np
from jax import lax
from jax.experimental import pallas as pl
from jax.experimental.pallas import tpu as pltpu
from jax.sharding import PartitionSpec as P

ND = 36
NF = 32
GW = 128


GRAV = 9.81
BASE_FREQ = 0.035
FREQ_RATIO = 1.1
CELL = 5000.0
STEP = 40.0
REFR_LIMIT = 0.5
WIND_RATE = 0.05
DISS_RATE = 0.3
NONLIN_RATE = 0.1


def extended_2(array, sides, width):
    for axis, dim in sides:
        size, length = (lax.axis_size(axis), array.shape[dim])
        up = [(i, (i + 1) % size) for i in range(size)]
        down = [(j, i) for i, j in up]
        last = lax.slice_in_dim(array, length - width, length, axis=dim)
        initial = lax.slice_in_dim(array, 0, width, axis=dim)
        before = lax.ppermute(last, axis, up)
        after = lax.ppermute(initial, axis, down)
        array = jnp.concatenate([before, array, after], axis=dim)
    return array


def bins(kidx):
    band = (kidx // ND).astype(jnp.float32)
    angle_id = (kidx % ND).astype(jnp.float32)
    sigma = 2.0 * math.pi * BASE_FREQ * FREQ_RATIO**band
    theta = 2.0 * math.pi * angle_id / ND
    return (sigma, jnp.cos(theta), jnp.sin(theta))


def wave_terms(sigma, water):
    scaled = sigma * sigma / GRAV * water
    kh = scaled / jnp.tanh(scaled**0.75) ** (2.0 / 3.0)
    decay = jnp.exp(-2.0 * kh)
    denom = 1.0 - decay * decay
    cphase = sigma * water / kh
    cgroup = 0.5 * cphase * (1.0 + 4.0 * kh * decay / denom)
    refr = 2.0 * sigma * decay / denom
    return (cphase, cgroup, refr)


def transport(energy, vel_x, vel_y, e_nb, v_nb, live):
    u_east = 0.5 * (vel_x + v_nb[0])
    f_east = live[0] * (jnp.maximum(u_east, 0.0) * energy + jnp.minimum(u_east, 0.0) * e_nb[0])
    u_west = 0.5 * (v_nb[1] + vel_x)
    f_west = live[1] * (jnp.maximum(u_west, 0.0) * e_nb[1] + jnp.minimum(u_west, 0.0) * energy)
    u_north = 0.5 * (vel_y + v_nb[2])
    f_north = live[2] * (jnp.maximum(u_north, 0.0) * energy + jnp.minimum(u_north, 0.0) * e_nb[2])
    u_south = 0.5 * (v_nb[3] + vel_y)
    f_south = live[3] * (jnp.maximum(u_south, 0.0) * e_nb[3] + jnp.minimum(u_south, 0.0) * energy)
    return energy - STEP / CELL * (f_east - f_west + f_north - f_south)


def sources(energy, water, grad_x, grad_y, wind, mask, interaction):
    total = NF * ND
    width = energy.shape[1]
    sigma, cosine, sine = bins(jnp.arange(total, dtype=jnp.int32))
    cphase, cgroup, refr = wave_terms(sigma[:, None], water[None, :])
    ctheta = -refr * (sine[:, None] * grad_x[None, :] - cosine[:, None] * grad_y[None, :])
    rate = jnp.clip(STEP / (2.0 * math.pi / ND) * ctheta, -REFR_LIMIT, REFR_LIMIT)
    rate3 = rate.reshape(NF, ND, width)
    energy3 = energy.reshape(NF, ND, width)
    face = 0.5 * (rate3 + jnp.roll(rate3, -1, axis=1))
    flow = jnp.maximum(face, 0.0) * energy3 + jnp.minimum(face, 0.0) * jnp.roll(energy3, -1, axis=1)
    refracted = (energy3 - (flow - jnp.roll(flow, 1, axis=1))).reshape(total, width)
    squared = refracted * refracted
    rms = jnp.sqrt(jnp.mean(squared, axis=0) + 1e-06)
    fbar = jnp.sum(sigma[:, None] * squared, axis=0) / (jnp.sum(squared, axis=0) + 1e-06)
    dissipation = DISS_RATE * (sigma[:, None] / fbar[None, :]) ** 2 * (rms / (1.0 + rms))[None, :]
    drive = (wind[0][None, :] * cosine[:, None] + wind[1][None, :] * sine[:, None]) / cphase - 1.0
    gain = WIND_RATE * sigma[:, None] * jnp.maximum(drive, 0.0)
    nonlinear = jnp.dot(
        interaction, squared.astype(jnp.bfloat16), preferred_element_type=jnp.float32
    )
    updated = refracted * (1.0 + gain) + NONLIN_RATE * nonlinear / rms[None, :]
    return mask.astype(jnp.float32)[None, :] * updated / (1.0 + dissipation)


def shifted(extended, tile_cells):
    return [
        extended[..., GW + 1 : GW + 1 + tile_cells],
        extended[..., GW - 1 : GW - 1 + tile_cells],
        extended[..., 2 * GW : 2 * GW + tile_cells],
        extended[..., 0:tile_cells],
    ]


def local(spectrum, depth, currents, winds, sea_mask, neighbours, interaction):
    comp_rows, tile_cells = spectrum.shape
    comp_id = lax.axis_index("comp")
    comp_count = lax.axis_size("comp")
    owned = tile_cells // comp_count
    empty = tile_cells + 2 * GW
    kidx = comp_id * comp_rows + jnp.arange(comp_rows, dtype=jnp.int32)
    sigma, cosine, sine = bins(kidx)
    cphase, cgroup, refr = wave_terms(sigma[:, None], depth[None, :])
    vel_x = cgroup * cosine[:, None] + currents[0][None, :]
    vel_y = cgroup * sine[:, None] + currents[1][None, :]
    stacked = jnp.concatenate([spectrum, vel_x, vel_y, depth[None, :]], axis=0)
    extended = extended_2(stacked, (("tile", 1),), GW)
    e_ext = extended[:comp_rows]
    vx_ext = extended[comp_rows : 2 * comp_rows]
    vy_ext = extended[2 * comp_rows : 3 * comp_rows]
    depth_ext = extended[3 * comp_rows]
    live = (neighbours != empty).astype(jnp.float32)
    e_nb = shifted(e_ext, tile_cells)
    vx_nb = shifted(vx_ext, tile_cells)
    vy_nb = shifted(vy_ext, tile_cells)
    v_nb = [vx_nb[0], vx_nb[1], vy_nb[2], vy_nb[3]]
    own_x = vx_ext[:, GW : GW + tile_cells]
    own_y = vy_ext[:, GW : GW + tile_cells]
    advected = transport(spectrum, own_x, own_y, e_nb, v_nb, live)
    depth_nb = shifted(depth_ext, tile_cells)
    near_depth = [jnp.where(live[j] > 0.0, depth_nb[j], depth) for j in range(4)]
    grad_x = (near_depth[0] - near_depth[1]) / (2.0 * CELL)
    grad_y = (near_depth[2] - near_depth[3]) / (2.0 * CELL)
    gathered = lax.all_to_all(advected, "comp", split_axis=1, concat_axis=0, tiled=True)
    start = comp_id * owned
    water = lax.dynamic_slice_in_dim(depth, start, owned, 0)
    slope_x = lax.dynamic_slice_in_dim(grad_x, start, owned, 0)
    slope_y = lax.dynamic_slice_in_dim(grad_y, start, owned, 0)
    wind = lax.dynamic_slice_in_dim(winds, start, owned, 1)
    mask = lax.dynamic_slice_in_dim(sea_mask, start, owned, 0)
    updated = sources(gathered, water, slope_x, slope_y, wind, mask, interaction)
    return lax.all_to_all(updated, "comp", split_axis=0, concat_axis=1, tiled=True)


def tables(comps, rows):
    angle = 2.0 * math.pi * (np.arange(rows) % ND) / ND
    sigma = 2.0 * math.pi * BASE_FREQ * FREQ_RATIO ** np.arange(NF, dtype=np.float64)
    bands = rows // ND
    by_comp = np.ones((comps, 8))
    by_comp[:, :bands] = sigma.reshape(comps, bands)
    lanes = np.ones((GW,))
    return (
        np.float32(np.cos(angle)[:, None] * lanes),
        np.float32(np.sin(angle)[:, None] * lanes),
        np.float32(by_comp[:, :, None] * lanes),
    )


def fits(comps, rows, cells):
    return rows % ND == 0 and rows % 16 == 0 and rows // ND <= 8 and cells == 2 * comps * GW and comps % 2 == 0


def wave_kernel(
    comps, tiles, rows,
    spec, depth, currents, winds, mask, neighbours, cosine, sine, sigmas, inter,
    out,
    field, cell, group, refr, slow, matrix, refracted, sq_send, sq_recv, nl_send, nl_recv, d_send, d_recv, half,
    in_sem, mat_sem, out_sem, halo_send, halo_recv, s1, r1, s2, r2, s3, r3,
):
    grid_rows = 2 * comps
    bands = rows // ND
    empty = grid_rows * GW + 2 * GW
    me = lax.axis_index("comp")
    tile = lax.axis_index("tile")
    later = lax.rem(tile + 1, tiles)
    earlier = lax.rem(tile + tiles - 1, tiles)
    f32 = jnp.float32

    barrier = pltpu.get_barrier_semaphore()
    for off in range(1, comps):
        pl.semaphore_signal(
            barrier, inc=1, device_id={"comp": lax.rem(me + off, comps)}, device_id_type=pl.DeviceIdType.MESH
        )
    for side in (later, earlier):
        pl.semaphore_signal(barrier, inc=1, device_id={"tile": side}, device_id_type=pl.DeviceIdType.MESH)

    def load(g):
        return pltpu.make_async_copy(spec.at[:, g * GW : (g + 1) * GW], field.at[g + 1], in_sem.at[g])

    for g in range(grid_rows):
        load(g).start()
    matrix_copy = pltpu.make_async_copy(inter, matrix, mat_sem)
    matrix_copy.start()

    sigma = sigmas[me]

    def waves(row):
        water = cell[row, 0:1, :]
        scaled = sigma * sigma * (1.0 / GRAV) * water
        kh = scaled * jnp.exp((-2.0 / 3.0) * jnp.log(jnp.tanh(jnp.sqrt(scaled * jnp.sqrt(scaled)))))
        decay = jnp.exp(-2.0 * kh)
        denom = 1.0 - decay * decay
        cphase = sigma * water / kh
        group[row] = 0.5 * cphase * (1.0 + 4.0 * kh * decay / denom)
        refr[row] = 2.0 * sigma * decay / denom
        slow[row] = kh / (sigma * water)

    for g in range(grid_rows):
        lanes = slice(g * GW, (g + 1) * GW)
        cell[g + 1, 0:1, :] = depth[:, lanes]
        cell[g + 1, 1:3, :] = currents[:, lanes]
        cell[g + 1, 3:5, :] = winds[:, lanes]
        cell[g + 1, 5:6, :] = mask[:, lanes].astype(f32)
        cell[g + 1, 6:8, :] = jnp.zeros((2, GW), f32)
    for g in range(grid_rows):
        waves(g + 1)

    for g in range(grid_rows):
        load(g).wait()
    pl.semaphore_wait(barrier, comps + 1)

    def halo(buffer, which):
        return (
            pltpu.make_async_remote_copy(
                src_ref=buffer.at[1], dst_ref=buffer.at[grid_rows + 1],
                send_sem=halo_send.at[which], recv_sem=halo_recv.at[which],
                device_id={"tile": earlier}, device_id_type=pl.DeviceIdType.MESH,
            ),
            pltpu.make_async_remote_copy(
                src_ref=buffer.at[grid_rows], dst_ref=buffer.at[0],
                send_sem=halo_send.at[which + 1], recv_sem=halo_recv.at[which + 1],
                device_id={"tile": later}, device_id_type=pl.DeviceIdType.MESH,
            ),
        )

    halos = halo(cell, 0) + halo(field, 2)
    for copy in halos:
        copy.start()

    row_of = lax.broadcasted_iota(jnp.int32, (rows, GW), 0)
    last_dir = functools.reduce(jnp.logical_or, [row_of == ND * b + ND - 1 for b in range(bands)])
    first_dir = functools.reduce(jnp.logical_or, [row_of == ND * b for b in range(bands)])
    lane = lax.broadcasted_iota(jnp.int32, (rows, GW), 1)
    lane8 = lax.broadcasted_iota(jnp.int32, (8, GW), 1)
    sub8 = lax.broadcasted_iota(jnp.int32, (8, GW), 0)

    def spread(c):
        by_band = [jnp.broadcast_to(c[b : b + 1], (8, GW)) for b in range(bands)]
        slabs = []
        for r in range(rows // 8):
            low, high = 8 * r // ND, (8 * r + 7) // ND
            if low == high:
                slabs.append(by_band[low])
            else:
                slabs.append(jnp.where(sub8 < ND * high - 8 * r, by_band[low], by_band[high]))
        return jnp.concatenate(slabs, axis=0)

    def along(x, following, lanes):
        return jnp.where(lanes == GW - 1, pltpu.roll(following, GW - 1, 1), pltpu.roll(x, GW - 1, 1))

    def back(x, preceding, lanes):
        return jnp.where(lanes == 0, pltpu.roll(preceding, 1, 1), pltpu.roll(x, 1, 1))

    def next_dir(x):
        return jnp.where(last_dir, pltpu.roll(x, ND - 1, 0), pltpu.roll(x, rows - 1, 0))

    def prev_dir(x):
        return jnp.where(first_dir, pltpu.roll(x, rows - ND + 1, 0), pltpu.roll(x, 1, 0))

    def grid_row(h, who):
        if h == 0:
            return comps // 2 + who
        return who + comps * (who // (comps // 2))

    def advance(g):
        e, e_n, e_s = field[g + 1], field[g + 2], field[g]
        nb = neighbours[:, pl.ds(pl.multiple_of(g * GW, GW), GW)]
        live = (nb != empty).astype(f32)
        c, c_n, c_s = cell[g + 1], cell[g + 2], cell[g]
        v, v_n, v_s = group[g + 1], group[g + 2], group[g]
        c_e, c_w = along(c, c_n, lane8), back(c, c_s, lane8)
        v_e, v_w = along(v, v_n, lane8), back(v, v_s, lane8)
        cos_k, sin_k = cosine[...], sine[...]

        def face(j, direction, axis, v_j, c_j):
            weight = (0.5 * STEP / CELL) * live[j : j + 1]
            wave = weight * (v + v_j)
            flow = weight * (c[axis : axis + 1] + c_j[axis : axis + 1])
            return direction * spread(wave) + flow

        u_e = face(0, cos_k, 1, v_e, c_e)
        u_w = face(1, cos_k, 1, v_w, c_w)
        u_n = face(2, sin_k, 2, v_n, c_n)
        u_s = face(3, sin_k, 2, v_s, c_s)
        f_e = jnp.maximum(u_e, 0.0) * e + jnp.minimum(u_e, 0.0) * along(e, e_n, lane)
        f_w = jnp.maximum(u_w, 0.0) * back(e, e_s, lane) + jnp.minimum(u_w, 0.0) * e
        f_n = jnp.maximum(u_n, 0.0) * e + jnp.minimum(u_n, 0.0) * e_n
        f_s = jnp.maximum(u_s, 0.0) * e_s + jnp.minimum(u_s, 0.0) * e
        adv = e - (f_e - f_w + f_n - f_s)

        h = c[0:1]
        near = [jnp.where(live[j : j + 1] > 0.0, x[0:1], h) for j, x in enumerate((c_e, c_w, c_n, c_s))]
        scale = (0.5 * STEP / (2.0 * math.pi / ND) / (2.0 * CELL)) * refr[g + 1]
        from_x = scale * (near[1] - near[0])
        from_y = scale * (near[2] - near[3])
        rate = jnp.clip(sin_k * spread(from_x) + cos_k * spread(from_y), -0.5 * REFR_LIMIT, 0.5 * REFR_LIMIT)
        m = rate + next_dir(rate)
        flow = jnp.maximum(m, 0.0) * adv + jnp.minimum(m, 0.0) * next_dir(adv)
        return adv - (flow - prev_dir(flow))

    def peer(s):
        return lax.rem(me + comps // 2 + s // 2 - (s % 2) * (2 * (s // 2) + 1) + comps, comps)

    def sender(s):
        return lax.rem(me + 2 * comps - (comps // 2 + s // 2 - (s % 2) * (2 * (s // 2) + 1)), comps)

    def first(h, who):
        return pltpu.make_async_remote_copy(
            src_ref=sq_send.at[h, who], dst_ref=sq_recv.at[h, me],
            send_sem=s1.at[h, who], recv_sem=r1.at[h, me],
            device_id={"comp": who}, device_id_type=pl.DeviceIdType.MESH,
        )

    def first_arrival(h, who):
        return pltpu.make_async_remote_copy(
            src_ref=sq_send.at[h, who], dst_ref=sq_recv.at[h, who],
            send_sem=s1.at[h, who], recv_sem=r1.at[h, who],
            device_id={"comp": who}, device_id_type=pl.DeviceIdType.MESH,
        )

    def second(h, who):
        return pltpu.make_async_remote_copy(
            src_ref=nl_send.at[h, who], dst_ref=nl_recv.at[h, me],
            send_sem=s2.at[h, who], recv_sem=r2.at[h, me],
            device_id={"comp": who}, device_id_type=pl.DeviceIdType.MESH,
        )

    def second_arrival(h, who):
        return pltpu.make_async_remote_copy(
            src_ref=nl_send.at[h, who], dst_ref=nl_recv.at[h, who],
            send_sem=s2.at[h, who], recv_sem=r2.at[h, who],
            device_id={"comp": who}, device_id_type=pl.DeviceIdType.MESH,
        )

    def third(h, who):
        return pltpu.make_async_remote_copy(
            src_ref=d_send.at[h], dst_ref=d_recv.at[h, me],
            send_sem=s3.at[h, who], recv_sem=r3.at[h, me],
            device_id={"comp": who}, device_id_type=pl.DeviceIdType.MESH,
        )

    def third_arrival(h, who):
        return pltpu.make_async_remote_copy(
            src_ref=d_send.at[h], dst_ref=d_recv.at[h, who],
            send_sem=s3.at[h, who], recv_sem=r3.at[h, who],
            device_id={"comp": who}, device_id_type=pl.DeviceIdType.MESH,
        )

    def store(who, g, h, target):
        r = advance(g)
        refracted[g] = r
        target[...] = r * r

    for h in range(2):
        if h == 1:
            for copy in halos:
                copy.wait()
            waves(0)
            waves(grid_rows + 1)

        def send(s, carry):
            who = peer(s)
            store(who, grid_row(h, who), h, sq_send.at[h, who])
            first(h, who).start()
            return carry

        lax.fori_loop(0, comps - 1, send, 0)
        store(me, grid_row(h, me), h, sq_recv.at[h, me])

    matrix_copy.wait()
    for h in range(2):
        def arrive(s, carry):
            first_arrival(h, sender(s)).wait_recv()
            return carry

        lax.fori_loop(0, comps - 1, arrive, 0)

        def add(who, sums):
            square = sq_recv[h, who]
            half[pl.ds(pl.multiple_of(who * rows, 16), rows), :] = square.astype(jnp.bfloat16)
            weighted = spread(sigmas[who]) * square
            return (
                sums[0] + jnp.sum(square.reshape(rows // 8, 8, GW), axis=0),
                sums[1] + jnp.sum(weighted.reshape(rows // 8, 8, GW), axis=0),
            )

        zero = jnp.zeros((8, GW), f32)
        total, moment = lax.fori_loop(0, comps, add, (zero, zero))
        total = jnp.sum(total, axis=0, keepdims=True)
        moment = jnp.sum(moment, axis=0, keepdims=True)
        rms = jnp.sqrt(total * (1.0 / (NF * ND)) + 1e-06)
        inverse = (total + 1e-06) / moment
        loss = DISS_RATE * inverse * inverse * (rms / (1.0 + rms))
        d_send[h] = loss
        d_recv[h, me] = loss
        scale = NONLIN_RATE / rms

        def product(who):
            part = matrix[pl.ds(pl.multiple_of(who * rows, 16), rows), :]
            return scale * jnp.dot(part, half[...], preferred_element_type=f32)

        def reply(s, carry):
            who = peer(s)
            nl_send[h, who] = product(who)
            second(h, who).start()
            third(h, who).start()
            return carry

        lax.fori_loop(0, comps - 1, reply, 0)
        nl_recv[h, me] = product(me)

    def finish(h, who):
        g = grid_row(h, who)
        c = cell[g + 1]
        keep = c[5:6] / (1.0 + sigma * sigma * d_recv[h, who])
        rate = WIND_RATE * sigma
        growth = rate * slow[g + 1]
        drive = cosine[...] * spread(growth * c[3:4]) + sine[...] * spread(growth * c[4:5])
        gain = jnp.maximum(drive - spread(rate), 0.0)
        r = refracted[g]
        refracted[g] = spread(keep) * (r * (1.0 + gain) + nl_recv[h, who])
        pltpu.make_async_copy(
            refracted.at[g], out.at[:, pl.ds(pl.multiple_of(g * GW, GW), GW)], out_sem.at[h, who]
        ).start()

    for h in range(2):
        finish(h, me)

        def complete(s, carry):
            who = sender(comps - 2 - s)
            second_arrival(h, who).wait_recv()
            third_arrival(h, who).wait_recv()
            finish(h, who)
            return carry

        lax.fori_loop(0, comps - 1, complete, 0)

    for h in range(2):
        def drain(s, carry):
            who = peer(s)
            first(h, who).wait_send()
            second(h, who).wait_send()
            third(h, who).wait_send()
            return carry

        lax.fori_loop(0, comps - 1, drain, 0)

        def written(who, carry):
            g = grid_row(h, who)
            pltpu.make_async_copy(
                refracted.at[g], out.at[:, pl.ds(pl.multiple_of(g * GW, GW), GW)], out_sem.at[h, who]
            ).wait()
            return carry

        lax.fori_loop(0, comps, written, 0)


def fused(spectrum, depth, currents, winds, sea_mask, neighbours, interaction):
    rows, cells = spectrum.shape
    comps, tiles = lax.axis_size("comp"), lax.axis_size("tile")
    grid_rows = cells // GW
    cosine, sine, sigmas = tables(comps, rows)
    vmem = pl.BlockSpec(memory_space=pltpu.VMEM)
    hbm = pl.BlockSpec(memory_space=pl.ANY)
    f32 = jnp.float32
    dma = pltpu.SemaphoreType.DMA
    return pl.pallas_call(
        functools.partial(wave_kernel, comps, tiles, rows),
        out_shape=jax.ShapeDtypeStruct((rows, cells), f32),
        in_specs=[hbm] + [vmem] * 8 + [hbm],
        out_specs=hbm,
        scratch_shapes=[
            pltpu.VMEM((grid_rows + 2, rows, GW), f32),
            pltpu.VMEM((grid_rows + 2, 8, GW), f32),
            pltpu.VMEM((grid_rows + 2, 8, GW), f32),
            pltpu.VMEM((grid_rows + 2, 8, GW), f32),
            pltpu.VMEM((grid_rows + 2, 8, GW), f32),
            pltpu.VMEM(interaction.shape, jnp.bfloat16),
            pltpu.VMEM((grid_rows, rows, GW), f32),
            pltpu.VMEM((2, comps, rows, GW), f32),
            pltpu.VMEM((2, comps, rows, GW), f32),
            pltpu.VMEM((2, comps, rows, GW), f32),
            pltpu.VMEM((2, comps, rows, GW), f32),
            pltpu.VMEM((2, 1, GW), f32),
            pltpu.VMEM((2, comps, 1, GW), f32),
            pltpu.VMEM((comps * rows, GW), jnp.bfloat16),
            dma((grid_rows,)),
            dma,
            dma((2, comps)),
            dma((4,)),
            dma((4,)),
            dma((2, comps)),
            dma((2, comps)),
            dma((2, comps)),
            dma((2, comps)),
            dma((2, comps)),
            dma((2, comps)),
        ],
        compiler_params=pltpu.CompilerParams(
            collective_id=0, has_side_effects=True, vmem_limit_bytes=32 * 1024 * 1024
        ),
        cost_estimate=pl.CostEstimate(
            flops=2 * cells // comps * (comps * rows) ** 2, bytes_accessed=8 * rows * cells, transcendentals=0
        ),
    )(
        spectrum, depth.reshape(1, cells), currents, winds, sea_mask.reshape(1, cells), neighbours,
        jnp.asarray(cosine), jnp.asarray(sine), jnp.asarray(sigmas), interaction,
    )


def step(spectrum, *rest):
    rows, cells = spectrum.shape
    if fits(lax.axis_size("comp"), rows, cells):
        return fused(spectrum, *rest)
    return local(spectrum, *rest)


def solution(mesh):
    return jax.shard_map(
        step,
        mesh=mesh,
        in_specs=(
            P("comp", "tile"),
            P("tile"),
            P(None, "tile"),
            P(None, "tile"),
            P("tile"),
            P(None, "tile"),
            P(),
        ),
        out_specs=P("comp", "tile"),
        check_vma=False,
    )
```

```python
import functools
import math

import jax
import jax.numpy as jnp
import numpy as np
from jax import lax
from jax.experimental import pallas as pl
from jax.experimental.pallas import tpu as pltpu
from jax.sharding import PartitionSpec as P

ND = 36
NF = 32
GW = 128


GRAV = 9.81
BASE_FREQ = 0.035
FREQ_RATIO = 1.1
CELL = 5000.0
STEP = 40.0
REFR_LIMIT = 0.5
WIND_RATE = 0.05
DISS_RATE = 0.3
NONLIN_RATE = 0.1


def extended_2(array, sides, width):
    for axis, dim in sides:
        size, length = (lax.axis_size(axis), array.shape[dim])
        up = [(i, (i + 1) % size) for i in range(size)]
        down = [(j, i) for i, j in up]
        last = lax.slice_in_dim(array, length - width, length, axis=dim)
        initial = lax.slice_in_dim(array, 0, width, axis=dim)
        before = lax.ppermute(last, axis, up)
        after = lax.ppermute(initial, axis, down)
        array = jnp.concatenate([before, array, after], axis=dim)
    return array


def bins(kidx):
    band = (kidx // ND).astype(jnp.float32)
    angle_id = (kidx % ND).astype(jnp.float32)
    sigma = 2.0 * math.pi * BASE_FREQ * FREQ_RATIO**band
    theta = 2.0 * math.pi * angle_id / ND
    return (sigma, jnp.cos(theta), jnp.sin(theta))


def wave_terms(sigma, water):
    scaled = sigma * sigma / GRAV * water
    kh = scaled / jnp.tanh(scaled**0.75) ** (2.0 / 3.0)
    decay = jnp.exp(-2.0 * kh)
    denom = 1.0 - decay * decay
    cphase = sigma * water / kh
    cgroup = 0.5 * cphase * (1.0 + 4.0 * kh * decay / denom)
    refr = 2.0 * sigma * decay / denom
    return (cphase, cgroup, refr)


def transport(energy, vel_x, vel_y, e_nb, v_nb, live):
    u_east = 0.5 * (vel_x + v_nb[0])
    f_east = live[0] * (jnp.maximum(u_east, 0.0) * energy + jnp.minimum(u_east, 0.0) * e_nb[0])
    u_west = 0.5 * (v_nb[1] + vel_x)
    f_west = live[1] * (jnp.maximum(u_west, 0.0) * e_nb[1] + jnp.minimum(u_west, 0.0) * energy)
    u_north = 0.5 * (vel_y + v_nb[2])
    f_north = live[2] * (jnp.maximum(u_north, 0.0) * energy + jnp.minimum(u_north, 0.0) * e_nb[2])
    u_south = 0.5 * (v_nb[3] + vel_y)
    f_south = live[3] * (jnp.maximum(u_south, 0.0) * e_nb[3] + jnp.minimum(u_south, 0.0) * energy)
    return energy - STEP / CELL * (f_east - f_west + f_north - f_south)


def sources(energy, water, grad_x, grad_y, wind, mask, interaction):
    total = NF * ND
    width = energy.shape[1]
    sigma, cosine, sine = bins(jnp.arange(total, dtype=jnp.int32))
    cphase, cgroup, refr = wave_terms(sigma[:, None], water[None, :])
    ctheta = -refr * (sine[:, None] * grad_x[None, :] - cosine[:, None] * grad_y[None, :])
    rate = jnp.clip(STEP / (2.0 * math.pi / ND) * ctheta, -REFR_LIMIT, REFR_LIMIT)
    rate3 = rate.reshape(NF, ND, width)
    energy3 = energy.reshape(NF, ND, width)
    face = 0.5 * (rate3 + jnp.roll(rate3, -1, axis=1))
    flow = jnp.maximum(face, 0.0) * energy3 + jnp.minimum(face, 0.0) * jnp.roll(energy3, -1, axis=1)
    refracted = (energy3 - (flow - jnp.roll(flow, 1, axis=1))).reshape(total, width)
    squared = refracted * refracted
    rms = jnp.sqrt(jnp.mean(squared, axis=0) + 1e-06)
    fbar = jnp.sum(sigma[:, None] * squared, axis=0) / (jnp.sum(squared, axis=0) + 1e-06)
    dissipation = DISS_RATE * (sigma[:, None] / fbar[None, :]) ** 2 * (rms / (1.0 + rms))[None, :]
    drive = (wind[0][None, :] * cosine[:, None] + wind[1][None, :] * sine[:, None]) / cphase - 1.0
    gain = WIND_RATE * sigma[:, None] * jnp.maximum(drive, 0.0)
    nonlinear = jnp.dot(
        interaction, squared.astype(jnp.bfloat16), preferred_element_type=jnp.float32
    )
    updated = refracted * (1.0 + gain) + NONLIN_RATE * nonlinear / rms[None, :]
    return mask.astype(jnp.float32)[None, :] * updated / (1.0 + dissipation)


def shifted(extended, tile_cells):
    return [
        extended[..., GW + 1 : GW + 1 + tile_cells],
        extended[..., GW - 1 : GW - 1 + tile_cells],
        extended[..., 2 * GW : 2 * GW + tile_cells],
        extended[..., 0:tile_cells],
    ]


def local(spectrum, depth, currents, winds, sea_mask, neighbours, interaction):
    comp_rows, tile_cells = spectrum.shape
    comp_id = lax.axis_index("comp")
    comp_count = lax.axis_size("comp")
    owned = tile_cells // comp_count
    empty = tile_cells + 2 * GW
    kidx = comp_id * comp_rows + jnp.arange(comp_rows, dtype=jnp.int32)
    sigma, cosine, sine = bins(kidx)
    cphase, cgroup, refr = wave_terms(sigma[:, None], depth[None, :])
    vel_x = cgroup * cosine[:, None] + currents[0][None, :]
    vel_y = cgroup * sine[:, None] + currents[1][None, :]
    stacked = jnp.concatenate([spectrum, vel_x, vel_y, depth[None, :]], axis=0)
    extended = extended_2(stacked, (("tile", 1),), GW)
    e_ext = extended[:comp_rows]
    vx_ext = extended[comp_rows : 2 * comp_rows]
    vy_ext = extended[2 * comp_rows : 3 * comp_rows]
    depth_ext = extended[3 * comp_rows]
    live = (neighbours != empty).astype(jnp.float32)
    e_nb = shifted(e_ext, tile_cells)
    vx_nb = shifted(vx_ext, tile_cells)
    vy_nb = shifted(vy_ext, tile_cells)
    v_nb = [vx_nb[0], vx_nb[1], vy_nb[2], vy_nb[3]]
    own_x = vx_ext[:, GW : GW + tile_cells]
    own_y = vy_ext[:, GW : GW + tile_cells]
    advected = transport(spectrum, own_x, own_y, e_nb, v_nb, live)
    depth_nb = shifted(depth_ext, tile_cells)
    near_depth = [jnp.where(live[j] > 0.0, depth_nb[j], depth) for j in range(4)]
    grad_x = (near_depth[0] - near_depth[1]) / (2.0 * CELL)
    grad_y = (near_depth[2] - near_depth[3]) / (2.0 * CELL)
    gathered = lax.all_to_all(advected, "comp", split_axis=1, concat_axis=0, tiled=True)
    start = comp_id * owned
    water = lax.dynamic_slice_in_dim(depth, start, owned, 0)
    slope_x = lax.dynamic_slice_in_dim(grad_x, start, owned, 0)
    slope_y = lax.dynamic_slice_in_dim(grad_y, start, owned, 0)
    wind = lax.dynamic_slice_in_dim(winds, start, owned, 1)
    mask = lax.dynamic_slice_in_dim(sea_mask, start, owned, 0)
    updated = sources(gathered, water, slope_x, slope_y, wind, mask, interaction)
    return lax.all_to_all(updated, "comp", split_axis=0, concat_axis=1, tiled=True)


def tables(comps, rows):
    angle = 2.0 * math.pi * (np.arange(rows) % ND) / ND
    sigma = 2.0 * math.pi * BASE_FREQ * FREQ_RATIO ** np.arange(NF, dtype=np.float64)
    bands = rows // ND
    by_comp = np.ones((comps, 8))
    by_comp[:, :bands] = sigma.reshape(comps, bands)
    lanes = np.ones((GW,))
    return (
        np.float32(np.cos(angle)[:, None] * lanes),
        np.float32(np.sin(angle)[:, None] * lanes),
        np.float32(by_comp[:, :, None] * lanes),
    )


def fits(comps, rows, cells):
    return rows % ND == 0 and rows % 16 == 0 and rows // ND <= 8 and cells == 2 * comps * GW and comps % 2 == 0


def wave_kernel(
    comps, tiles, rows,
    spec, inter, *refs,
):
    inputs, refs = refs[:8], refs[8:]
    out, (depth, currents, winds, mask, neighbours, cosine, sine, sigmas), refs = refs[0], refs[1:9], refs[9:]
    (
    field, cell, group, refr, slow, matrix, refracted, sq_send, sq_recv, nl_send, nl_recv, d_send, d_recv, half,
    in_sem, small_sem, mat_sem, out_sem, halo_send, halo_recv, s1, r1, s2, r2, s3, r3,
    ) = refs
    grid_rows = 2 * comps
    bands = rows // ND
    empty = grid_rows * GW + 2 * GW
    me = lax.axis_index("comp")
    tile = lax.axis_index("tile")
    later = lax.rem(tile + 1, tiles)
    earlier = lax.rem(tile + tiles - 1, tiles)
    f32 = jnp.float32

    barrier = pltpu.get_barrier_semaphore()
    for off in range(1, comps):
        pl.semaphore_signal(
            barrier, inc=1, device_id={"comp": lax.rem(me + off, comps)}, device_id_type=pl.DeviceIdType.MESH
        )
    for side in (later, earlier):
        pl.semaphore_signal(barrier, inc=1, device_id={"tile": side}, device_id_type=pl.DeviceIdType.MESH)

    def load(g):
        return pltpu.make_async_copy(spec.at[:, g * GW : (g + 1) * GW], field.at[g + 1], in_sem.at[g])

    smalls = [
        pltpu.make_async_copy(source, target, small_sem.at[i])
        for i, (source, target) in enumerate(
            zip(inputs, (depth, currents, winds, mask, neighbours, cosine, sine, sigmas))
        )
    ]
    for copy in smalls:
        copy.start()
    for g in range(grid_rows):
        load(g).start()
    matrix_copy = pltpu.make_async_copy(inter, matrix, mat_sem)
    matrix_copy.start()
    for copy in smalls:
        copy.wait()

    sigma = sigmas[me]

    def waves(row):
        water = cell[row, 0:1, :]
        scaled = sigma * sigma * (1.0 / GRAV) * water
        kh = scaled * jnp.exp((-2.0 / 3.0) * jnp.log(jnp.tanh(jnp.sqrt(scaled * jnp.sqrt(scaled)))))
        decay = jnp.exp(-2.0 * kh)
        denom = 1.0 - decay * decay
        cphase = sigma * water / kh
        group[row] = 0.5 * cphase * (1.0 + 4.0 * kh * decay / denom)
        refr[row] = 2.0 * sigma * decay / denom
        slow[row] = kh / (sigma * water)

    for g in range(grid_rows):
        lanes = slice(g * GW, (g + 1) * GW)
        cell[g + 1, 0:1, :] = depth[:, lanes]
        cell[g + 1, 1:3, :] = currents[:, lanes]
        cell[g + 1, 3:5, :] = winds[:, lanes]
        cell[g + 1, 5:6, :] = mask[:, lanes].astype(f32)
        cell[g + 1, 6:8, :] = jnp.zeros((2, GW), f32)
    for g in range(grid_rows):
        waves(g + 1)

    for g in range(grid_rows):
        load(g).wait()

    def halo(buffer, which):
        return (
            pltpu.make_async_remote_copy(
                src_ref=buffer.at[1], dst_ref=buffer.at[grid_rows + 1],
                send_sem=halo_send.at[which], recv_sem=halo_recv.at[which],
                device_id={"tile": earlier}, device_id_type=pl.DeviceIdType.MESH,
            ),
            pltpu.make_async_remote_copy(
                src_ref=buffer.at[grid_rows], dst_ref=buffer.at[0],
                send_sem=halo_send.at[which + 1], recv_sem=halo_recv.at[which + 1],
                device_id={"tile": later}, device_id_type=pl.DeviceIdType.MESH,
            ),
        )

    halos = halo(cell, 0) + halo(field, 2)

    row_of = lax.broadcasted_iota(jnp.int32, (rows, GW), 0)
    last_dir = functools.reduce(jnp.logical_or, [row_of == ND * b + ND - 1 for b in range(bands)])
    first_dir = functools.reduce(jnp.logical_or, [row_of == ND * b for b in range(bands)])
    lane = lax.broadcasted_iota(jnp.int32, (rows, GW), 1)
    lane8 = lax.broadcasted_iota(jnp.int32, (8, GW), 1)
    sub8 = lax.broadcasted_iota(jnp.int32, (8, GW), 0)

    def spread(c):
        by_band = [jnp.broadcast_to(c[b : b + 1], (8, GW)) for b in range(bands)]
        slabs = []
        for r in range(rows // 8):
            low, high = 8 * r // ND, (8 * r + 7) // ND
            if low == high:
                slabs.append(by_band[low])
            else:
                slabs.append(jnp.where(sub8 < ND * high - 8 * r, by_band[low], by_band[high]))
        return jnp.concatenate(slabs, axis=0)

    def along(x, following, lanes):
        return jnp.where(lanes == GW - 1, pltpu.roll(following, GW - 1, 1), pltpu.roll(x, GW - 1, 1))

    def back(x, preceding, lanes):
        return jnp.where(lanes == 0, pltpu.roll(preceding, 1, 1), pltpu.roll(x, 1, 1))

    def next_dir(x):
        return jnp.where(last_dir, pltpu.roll(x, ND - 1, 0), pltpu.roll(x, rows - 1, 0))

    def prev_dir(x):
        return jnp.where(first_dir, pltpu.roll(x, rows - ND + 1, 0), pltpu.roll(x, 1, 0))

    def grid_row(h, who):
        if h == 0:
            return comps // 2 + who
        return who + comps * (who // (comps // 2))

    def advance(g):
        e, e_n, e_s = field[g + 1], field[g + 2], field[g]
        nb = neighbours[:, pl.ds(pl.multiple_of(g * GW, GW), GW)]
        live = (nb != empty).astype(f32)
        c, c_n, c_s = cell[g + 1], cell[g + 2], cell[g]
        v, v_n, v_s = group[g + 1], group[g + 2], group[g]
        c_e, c_w = along(c, c_n, lane8), back(c, c_s, lane8)
        v_e, v_w = along(v, v_n, lane8), back(v, v_s, lane8)
        cos_k, sin_k = cosine[...], sine[...]

        def face(j, direction, axis, v_j, c_j):
            weight = (0.5 * STEP / CELL) * live[j : j + 1]
            wave = weight * (v + v_j)
            flow = weight * (c[axis : axis + 1] + c_j[axis : axis + 1])
            return direction * spread(wave) + flow

        u_e = face(0, cos_k, 1, v_e, c_e)
        u_w = face(1, cos_k, 1, v_w, c_w)
        u_n = face(2, sin_k, 2, v_n, c_n)
        u_s = face(3, sin_k, 2, v_s, c_s)
        f_e = jnp.maximum(u_e, 0.0) * e + jnp.minimum(u_e, 0.0) * along(e, e_n, lane)
        f_w = jnp.maximum(u_w, 0.0) * back(e, e_s, lane) + jnp.minimum(u_w, 0.0) * e
        f_n = jnp.maximum(u_n, 0.0) * e + jnp.minimum(u_n, 0.0) * e_n
        f_s = jnp.maximum(u_s, 0.0) * e_s + jnp.minimum(u_s, 0.0) * e
        adv = e - (f_e - f_w + f_n - f_s)

        h = c[0:1]
        near = [jnp.where(live[j : j + 1] > 0.0, x[0:1], h) for j, x in enumerate((c_e, c_w, c_n, c_s))]
        scale = (0.5 * STEP / (2.0 * math.pi / ND) / (2.0 * CELL)) * refr[g + 1]
        from_x = scale * (near[1] - near[0])
        from_y = scale * (near[2] - near[3])
        rate = jnp.clip(sin_k * spread(from_x) + cos_k * spread(from_y), -0.5 * REFR_LIMIT, 0.5 * REFR_LIMIT)
        m = rate + next_dir(rate)
        flow = jnp.maximum(m, 0.0) * adv + jnp.minimum(m, 0.0) * next_dir(adv)
        return adv - (flow - prev_dir(flow))

    side = comps // 2
    mine = (me // side) * side

    def peer(s):
        return lax.rem(me + comps // 2 + s // 2 - (s % 2) * (2 * (s // 2) + 1) + comps, comps)

    def sender(s):
        return lax.rem(me + 2 * comps - (comps // 2 + s // 2 - (s % 2) * (2 * (s // 2) + 1)), comps)

    def first(h, who):
        return pltpu.make_async_remote_copy(
            src_ref=sq_send.at[h, who], dst_ref=sq_recv.at[h, me],
            send_sem=s1.at[h, who], recv_sem=r1.at[h, me],
            device_id={"comp": who}, device_id_type=pl.DeviceIdType.MESH,
        )

    def first_arrival(h, who):
        return pltpu.make_async_remote_copy(
            src_ref=sq_send.at[h, who], dst_ref=sq_recv.at[h, who],
            send_sem=s1.at[h, who], recv_sem=r1.at[h, who],
            device_id={"comp": who}, device_id_type=pl.DeviceIdType.MESH,
        )

    def second(h, who):
        return pltpu.make_async_remote_copy(
            src_ref=nl_send.at[h, who], dst_ref=nl_recv.at[h, me],
            send_sem=s2.at[h, who], recv_sem=r2.at[h, me],
            device_id={"comp": who}, device_id_type=pl.DeviceIdType.MESH,
        )

    def second_arrival(h, who):
        return pltpu.make_async_remote_copy(
            src_ref=nl_send.at[h, who], dst_ref=nl_recv.at[h, who],
            send_sem=s2.at[h, who], recv_sem=r2.at[h, who],
            device_id={"comp": who}, device_id_type=pl.DeviceIdType.MESH,
        )

    def third(h, who):
        return pltpu.make_async_remote_copy(
            src_ref=d_send.at[h], dst_ref=d_recv.at[h, me],
            send_sem=s3.at[h, who], recv_sem=r3.at[h, me],
            device_id={"comp": who}, device_id_type=pl.DeviceIdType.MESH,
        )

    def third_arrival(h, who):
        return pltpu.make_async_remote_copy(
            src_ref=d_send.at[h], dst_ref=d_recv.at[h, who],
            send_sem=s3.at[h, who], recv_sem=r3.at[h, who],
            device_id={"comp": who}, device_id_type=pl.DeviceIdType.MESH,
        )

    def store(who, g, h, target):
        r = advance(g)
        refracted[g] = r
        target[...] = r * r

    for h in range(2):
        if h == 1:
            for copy in halos:
                copy.wait()
            waves(0)
            waves(grid_rows + 1)

        def send(s, carry):
            who = peer(s)
            store(who, grid_row(h, who), h, sq_send.at[h, who])
            if h == 0:
                @pl.when(s == 0)
                def _():
                    pl.semaphore_wait(barrier, comps + 1)

            first(h, who).start()
            if h == 0:
                @pl.when(s == 0)
                def _():
                    for copy in halos:
                        copy.start()

            return carry

        lax.fori_loop(0, comps - 1, send, 0)
        store(me, grid_row(h, me), h, sq_recv.at[h, me])

    matrix_copy.wait()
    for h in range(2):
        def arrive(s, carry):
            first_arrival(h, sender(s)).wait_recv()
            return carry

        lax.fori_loop(0, comps - 1, arrive, 0)

        def add(who, sums):
            square = sq_recv[h, who]
            half[pl.ds(pl.multiple_of(who * rows, 16), rows), :] = square.astype(jnp.bfloat16)
            weighted = spread(sigmas[who]) * square
            return (
                sums[0] + jnp.sum(square.reshape(rows // 8, 8, GW), axis=0),
                sums[1] + jnp.sum(weighted.reshape(rows // 8, 8, GW), axis=0),
            )

        zero = jnp.zeros((8, GW), f32)
        total, moment = lax.fori_loop(0, comps, add, (zero, zero))
        total = jnp.sum(total, axis=0, keepdims=True)
        moment = jnp.sum(moment, axis=0, keepdims=True)
        rms = jnp.sqrt(total * (1.0 / (NF * ND)) + 1e-06)
        inverse = (total + 1e-06) / moment
        loss = DISS_RATE * inverse * inverse * (rms / (1.0 + rms))
        d_send[h] = loss
        d_recv[h, me] = loss
        scale = NONLIN_RATE / rms

        def product(who):
            part = matrix[pl.ds(pl.multiple_of(who * rows, 16), rows), :]
            return scale * jnp.dot(part, half[...], preferred_element_type=f32)

        def reply(s, carry):
            who = lax.rem(me + 1 + s, comps)
            nl_send[h, who] = product(who)
            second(h, who).start()
            third(h, who).start()
            return carry

        lax.fori_loop(0, comps - 1, reply, 0)
        nl_recv[h, me] = product(me)

    def finish(h, who):
        g = grid_row(h, who)
        c = cell[g + 1]
        keep = c[5:6] / (1.0 + sigma * sigma * d_recv[h, who])
        rate = WIND_RATE * sigma
        growth = rate * slow[g + 1]
        drive = cosine[...] * spread(growth * c[3:4]) + sine[...] * spread(growth * c[4:5])
        gain = jnp.maximum(drive - spread(rate), 0.0)
        r = refracted[g]
        refracted[g] = spread(keep) * (r * (1.0 + gain) + nl_recv[h, who])
        pltpu.make_async_copy(
            refracted.at[g], out.at[:, pl.ds(pl.multiple_of(g * GW, GW), GW)], out_sem.at[h, who]
        ).start()

    for h in range(2):
        finish(h, me)

        def complete(s, carry):
            who = lax.rem(me + comps - 1 - s, comps)
            second_arrival(h, who).wait_recv()
            third_arrival(h, who).wait_recv()
            finish(h, who)
            return carry

        lax.fori_loop(0, comps - 1, complete, 0)

    for h in range(2):
        def drain(s, carry):
            who = peer(s)
            first(h, who).wait_send()
            second(h, who).wait_send()
            third(h, who).wait_send()
            return carry

        lax.fori_loop(0, comps - 1, drain, 0)

        def written(who, carry):
            g = grid_row(h, who)
            pltpu.make_async_copy(
                refracted.at[g], out.at[:, pl.ds(pl.multiple_of(g * GW, GW), GW)], out_sem.at[h, who]
            ).wait()
            return carry

        lax.fori_loop(0, comps, written, 0)


def fused(spectrum, depth, currents, winds, sea_mask, neighbours, interaction):
    rows, cells = spectrum.shape
    comps, tiles = lax.axis_size("comp"), lax.axis_size("tile")
    grid_rows = cells // GW
    cosine, sine, sigmas = tables(comps, rows)
    hbm = pl.BlockSpec(memory_space=pltpu.HBM)
    small = (
        depth.reshape(1, cells), currents, winds, sea_mask.reshape(1, cells), neighbours,
        jnp.asarray(cosine), jnp.asarray(sine), jnp.asarray(sigmas),
    )
    f32 = jnp.float32
    dma = pltpu.SemaphoreType.DMA
    return pl.pallas_call(
        functools.partial(wave_kernel, comps, tiles, rows),
        out_shape=jax.ShapeDtypeStruct((rows, cells), f32),
        in_specs=[hbm] * 10,
        out_specs=hbm,
        scratch_shapes=[pltpu.VMEM(x.shape, x.dtype) for x in small] + [
            pltpu.VMEM((grid_rows + 2, rows, GW), f32),
            pltpu.VMEM((grid_rows + 2, 8, GW), f32),
            pltpu.VMEM((grid_rows + 2, 8, GW), f32),
            pltpu.VMEM((grid_rows + 2, 8, GW), f32),
            pltpu.VMEM((grid_rows + 2, 8, GW), f32),
            pltpu.VMEM(interaction.shape, jnp.bfloat16),
            pltpu.VMEM((grid_rows, rows, GW), f32),
            pltpu.VMEM((2, comps, rows, GW), f32),
            pltpu.VMEM((2, comps, rows, GW), f32),
            pltpu.VMEM((2, comps, rows, GW), f32),
            pltpu.VMEM((2, comps, rows, GW), f32),
            pltpu.VMEM((2, 1, GW), f32),
            pltpu.VMEM((2, comps, 1, GW), f32),
            pltpu.VMEM((comps * rows, GW), jnp.bfloat16),
            dma((grid_rows,)),
            dma((8,)),
            dma,
            dma((2, comps)),
            dma((4,)),
            dma((4,)),
            dma((2, comps)),
            dma((2, comps)),
            dma((2, comps)),
            dma((2, comps)),
            dma((2, comps)),
            dma((2, comps)),
        ],
        compiler_params=pltpu.CompilerParams(
            collective_id=0, has_side_effects=True, vmem_limit_bytes=60 * 1024 * 1024
        ),
        cost_estimate=pl.CostEstimate(
            flops=2 * cells // comps * (comps * rows) ** 2, bytes_accessed=8 * rows * cells, transcendentals=0
        ),
    )(
        spectrum, interaction, *small,
    )


def step(spectrum, *rest):
    rows, cells = spectrum.shape
    if fits(lax.axis_size("comp"), rows, cells):
        return fused(spectrum, *rest)
    return local(spectrum, *rest)


def solution(mesh):
    return jax.shard_map(
        step,
        mesh=mesh,
        in_specs=(
            P("comp", "tile"),
            P("tile"),
            P(None, "tile"),
            P(None, "tile"),
            P("tile"),
            P(None, "tile"),
            P(),
        ),
        out_specs=P("comp", "tile"),
        check_vma=False,
    )
```
